256 devices in a mesh: expert: 8 (over y, core), blk: 16 (over x, z_hi), dp: 2 (over z_lo).
Axes of the slice: x: 4, y: 4, z: 8 (z_hi: 4, z_lo: 2; z = z_hi * 2 + z_lo), core: 2. Of those that a mesh axis runs over, the one named last changes fastest.
Arguments:
- tokens: bfloat16 [2048, 7168], P(('expert', 'dp'), 'blk'), may hold values from -6 to 6
- row_scales: bfloat16 [2048], P(('expert', 'dp')), may hold values from 0.75 to 1.25
- chosen: int32 [8, 512], P('expert'), may hold values from 0 to 2047, as said below
- combine: float32 [8, 512], P('expert'), may hold values from 0.6 to 1
- gate_weight: bfloat16 [8, 7168, 9216], P('expert', None, ('blk', 'dp')), may hold values from -0.0625 to 0.0625
- up_weight: bfloat16 [8, 7168, 9216], P('expert', None, ('blk', 'dp')), may hold values from -0.0625 to 0.0625
- down_weight: bfloat16 [8, 9216, 7168], P('expert', ('blk', 'dp')), may hold values from -0.0625 to 0.0625
Outputs:
- mixed: bfloat16 [2048, 7168], P(('expert', 'dp'), 'blk')
The draws below stay inside these ranges and needn't reach their ends.
Inputs may be any that keep to these rules, and one draw needn't show every extreme that they name: `chosen`: each row names 512 different tokens.
All inputs are finite; a program needn't handle non-finite values.
Results may differ from the reference program's by a relative error of at most 0.023.
Values may be sent and summed in bfloat16 or wider, within the bound.
No kernel may reach another device: no remote copies, remote signals or barrier semaphores. Data moves between devices by JAX's collectives and lax.ppermute only.
A program may use at most 128 MiB of HBM per device.

```python
import jax
import jax.numpy as jnp
from jax import lax

D = 7168
FF = 9216
EXPERTS = 8
TOKENS = 2048
CAP = 512
N_BLK = 16
N_DP = 2


def draw_chosen(key, part):
    key = jax.random.fold_in(key, 7)
    keys = jax.random.split(key, EXPERTS)
    orders = jax.vmap(lambda single: jax.random.permutation(single, TOKENS))(keys).astype(jnp.int32)
    targets = jnp.where(jnp.arange(EXPERTS) == 0, TOKENS - 1, 0).astype(jnp.int32)
    places = jnp.argmax(orders == targets[:, None], axis=1).astype(jnp.int32)
    rolled = jax.vmap(lambda order, place: jnp.roll(order, -place))(orders, places)
    return rolled[:, :CAP].astype(jnp.int32)


def block_levels(rng, dims, cuts, low, largest):
    level, own = 1.0, jax.random.fold_in(rng, 6)
    for axis_at, parts in cuts:
        steps = jnp.exp(jax.random.uniform(jax.random.fold_in(own, axis_at), (parts,), jnp.float32, low / len(cuts), largest / len(cuts)))
        level = level * jnp.repeat(steps, dims[axis_at] // parts).reshape([-1 if axis == axis_at else 1 for axis in range(len(dims))])
    return level


def bell_draw(rng, dims, scale, limit, cuts=(), kind=jnp.bfloat16):
    entries = scale * jax.random.normal(rng, dims, jnp.float32)
    if cuts:
        entries = entries * block_levels(rng, dims, cuts, -0.22, 0.18)
    return jnp.clip(entries, -limit, limit).astype(kind)


def setup_inputs(seed: int = 0) -> dict:
    key_list = jax.random.split(jax.random.key(seed), 8)
    tokens = bell_draw(key_list[0], (TOKENS, D), 1.0, 6.0, ((0, 16), (1, 16)))
    row_scales = jnp.clip(0.75 + 0.5 * jax.random.uniform(key_list[1], (TOKENS,), jnp.float32) ** block_levels(key_list[1], (TOKENS,), ((0, 16),), -0.2, 0.2), 0.75, 1.25).astype(jnp.bfloat16)
    chosen = draw_chosen(jax.random.fold_in(key_list[7], 71), 0)
    combine = jnp.clip(0.6 + 0.39999998 * jax.random.uniform(key_list[3], (EXPERTS, CAP), jnp.float32) ** block_levels(key_list[3], (EXPERTS, CAP), ((0, 8),), -0.2, 0.2), 0.6, 1.0)
    gate_weight = bell_draw(key_list[4], (EXPERTS, D, FF), D ** -0.5, 0.0625, ((0, 8), (2, 32)))
    up_weight = bell_draw(key_list[5], (EXPERTS, D, FF), D ** -0.5, 0.0625, ((0, 8), (2, 32)))
    down_weight = bell_draw(key_list[6], (EXPERTS, FF, D), FF ** -0.5, 0.0625, ((0, 8), (1, 32)))
    return dict(tokens=tokens, row_scales=row_scales, chosen=chosen, combine=combine, gate_weight=gate_weight, up_weight=up_weight, down_weight=down_weight)


def reference(tokens, row_scales, chosen, combine, gate_weight, up_weight, down_weight):
    slices = N_BLK * N_DP
    width = FF // slices
    total = jnp.zeros((TOKENS, D), jnp.float32)
    for expert in range(EXPERTS):
        index = chosen[expert]
        rows = tokens[index].astype(jnp.float32) * row_scales[index].astype(jnp.float32)[:, None]
        selected = rows.astype(jnp.bfloat16)
        gate = jnp.dot(selected, gate_weight[expert], preferred_element_type=jnp.float32)
        up = jnp.dot(selected, up_weight[expert], preferred_element_type=jnp.float32)
        hidden = (jax.nn.silu(gate) * up).astype(jnp.bfloat16)
        down_slab = down_weight[expert]

        def add_slice(running, number):
            start = (number * width).astype(jnp.int32)
            part_hidden = lax.dynamic_slice_in_dim(hidden, start, width, 1)
            part_down = lax.dynamic_slice_in_dim(down_slab, start, width, 0)
            term = jnp.dot(part_hidden, part_down, preferred_element_type=jnp.float32).astype(jnp.bfloat16)
            term = lax.optimization_barrier(term)
            return running + term.astype(jnp.float32), None

        expert_out, _ = lax.scan(add_slice, jnp.zeros((CAP, D), jnp.float32), jnp.arange(slices, dtype=jnp.int32))
        total = total.at[index].add(combine[expert][:, None] * expert_out)
    return total.astype(jnp.bfloat16)
```

```python
import jax
import jax.numpy as jnp
from jax import lax
from jax.sharding import PartitionSpec as P

F32, BF16 = jnp.float32, jnp.bfloat16
AXES = ("expert", "blk", "dp")
NY, NC, NX, NZ = 4, 2, 4, 8
PARTS = 2


def pairs(move0, move1):
    out = []
    for y in range(NY):
        for c, move in ((0, move0), (1, move1)):
            if move is None:
                continue
            dy, dc, dx, dz = move
            for x in range(NX):
                for z in range(NZ):
                    source = ((y * NC + c) * NX + x) * NZ + z
                    target = (((y + dy) % NY * NC + (c ^ dc)) * NX + (x + dx) % NX) * NZ + (z + dz) % NZ
                    out.append((source, target))
    return out


def send(a, move0, move1):
    return lax.ppermute(a, AXES, pairs(move0, move1))


def mx(d):
    return (0, 0, d, 0)


def mz(d):
    return (0, 0, 0, d)


def my(d):
    return (d, 0, 0, 0)


def cat(*a):
    return jnp.concatenate(a, axis=0)


NEAR = (0, -1, 1, -2)
FAR = (2, -3, 3, 4)


def tables(x, z, core):
    def c0(d):
        return [((x + i) % NX) * NZ + (z + d) % NZ for i in NEAR]

    def c1(d, zs):
        return [((x + d) % NX) * NZ + (z + i) % NZ for i in zs]

    def pick(a, b):
        return [jnp.where(core == 0, p, q) for p, q in zip(a, b)]

    gather = [
        pick(c0(0), c1(0, NEAR)),
        pick(c0(-1), c1(-1, NEAR)),
        pick(c0(1), c1(1, NEAR)),
        pick(c0(-2), c1(-1, FAR)),
        pick(c0(2), c1(1, FAR)),
        pick(c0(-3), c1(2, NEAR)),
        pick(c0(3), c1(2, FAR)),
        pick(c0(4), c1(0, FAR)),
    ]
    scatter = dict(
        home=pick(c0(0), c1(0, NEAR)),
        last=pick(c0(4), c1(0, FAR)),
        p2=pick(c0(3), c1(2, FAR)),
        m2=pick(c0(-3), c1(-1, FAR)),
        p3=pick(c0(2), c1(1, FAR)),
        m3=pick(c0(-2), c1(2, NEAR)),
        p4=pick(c0(1), c1(1, NEAR)),
        m4=pick(c0(-1), c1(-1, NEAR)),
    )
    return gather, scatter


def gather_plane(p, core0):
    n = p.shape[0]
    h = n // 32 * 16
    r1 = send(p, mx(1), mz(1))
    r2 = send(p, mx(-1), mz(-1))
    r3 = send(p, mx(2), mz(2))
    r4 = send(p, None, mz(-2))
    near = cat(p, r1, r2, r3)
    a1 = send(near, mz(1), mx(1))
    b1 = send(near, mz(-1), mx(-1))
    f1 = send(r3, None, mz(1))
    f2 = send(r4, None, mz(-1))
    f3 = send(r3[:h], None, mz(2))
    f4 = send(r4[h:], None, mz(-2))
    far = cat(r4, f1, f2, f3, f4)
    a2 = send(jnp.where(core0, a1, far), mz(1), mx(1))
    b2 = send(jnp.where(core0, b1, far), mz(-1), mx(-1))
    a3 = send(jnp.where(core0, a2, a1), mz(1), mx(1))
    b3 = send(b2, mz(-1), mx(-1))
    a4 = send(a3[: 2 * n], mz(1), None)
    b4 = send(b3[2 * n :], mz(-1), None)
    last = jnp.where(core0, cat(a4, b4), far)
    return [near, a1, b1, a2, b2, a3, b3, last]


def add(*a):
    total = a[0].astype(F32)
    for v in a[1:]:
        total = total + v.astype(F32)
    return total.astype(BF16)


def scatter_plane(blocks, core0):
    n = blocks["home"].shape[0] // 4
    h = n // 32 * 16
    last = blocks["last"]
    zero2 = jnp.zeros_like(last[: 2 * n])
    p1 = send(last[: 2 * n], mz(1), None)
    m1 = send(last[2 * n :], mz(-1), None)
    p2 = send(add(blocks["p2"], cat(p1, zero2)), mz(1), mx(1))
    m2 = send(add(blocks["m2"], cat(zero2, m1)), mz(-1), mx(-1))
    p3 = send(add(blocks["p3"], p2), mz(1), mx(1))
    m3 = send(add(blocks["m3"], jnp.where(core0, m2, 0)), mz(-1), mx(-1))
    p4 = send(add(blocks["p4"], jnp.where(core0, p3, 0)), mz(1), mx(1))
    m4 = send(add(blocks["m4"], m3), mz(-1), mx(-1))
    far = add(last, p3, m2)
    f1 = send(far[2 * n : 3 * n], None, mz(1))
    f2 = send(far[n : 2 * n], None, mz(-1))
    f3 = send(far[3 * n : 3 * n + h], None, mz(2))
    f4 = send(far[3 * n + h :], None, mz(-2))
    near = add(blocks["home"], p4, m4)
    s1 = send(near[2 * n : 3 * n], mx(1), mz(1))
    s2 = send(near[n : 2 * n], mx(-1), mz(-1))
    z1, z2 = jnp.zeros_like(f3), jnp.zeros_like(f4)
    s3 = send(add(jnp.where(core0, near[3 * n :], far[:n]), f1, cat(f3, z2)), mx(2), mz(2))
    s4 = send(add(near[3 * n :], f2, cat(z1, f4)), None, mz(-2))
    return sum(v.astype(F32) for v in (near[:n], s1, s2, s3, s4))


def shards(tokens, row_scales, chosen, combine, gate_weight, up_weight, down_weight):
    expert = lax.axis_index("expert")
    y, core = expert // NC, expert % NC
    dp = lax.axis_index("dp")
    place = lax.axis_index(("blk", "dp"))
    x, z = place // NZ, place % NZ
    core0 = core == 0
    swap_dp = [(0, 1), (1, 0)]
    block, features = tokens.shape
    half = features // 2
    picks, share = chosen[0], combine[0]
    slots = picks.shape[0]
    width = slots // PARTS
    order_y = (0, -1, 1, 2)

    scaled = (tokens.astype(F32) * row_scales.astype(F32)[:, None]).astype(BF16).T
    mine = lax.dynamic_slice_in_dim(scaled, dp * half, half, 0)
    theirs = lax.dynamic_slice_in_dim(scaled, (1 - dp) * half, half, 0)
    pair = jnp.concatenate([mine, lax.ppermute(theirs, "dp", swap_dp)], axis=1)
    column = jnp.concatenate([pair] + [send(pair, my(-d), my(-d)) for d in order_y[1:]], axis=1)
    rows = jnp.concatenate([column, send(column, (0, 1, 0, 0), (0, 1, 0, 0))], axis=1)
    firsts = [
        ((((y + d) % NY) * NC + (core ^ c)) * 2 + (dp ^ j)) * block
        for c in range(NC)
        for d in order_y
        for j in range(2)
    ]
    ids = (jnp.stack(firsts)[:, None] + jnp.arange(block)[None, :]).reshape(-1)
    onehot = (ids[:, None] == picks[None, :]).astype(BF16)

    gather, scatter = tables(x, z, core)
    contract = (((0,), (0,)), ((), ()))
    sums = []
    for part in range(PARTS):
        cols = slice(part * width, (part + 1) * width)
        piece = jnp.dot(rows, onehot[:, cols], preferred_element_type=F32).astype(BF16)
        blocks = gather_plane(piece, core0)
        whole = jnp.zeros((NX * NZ * half, width), BF16)
        for table, got in zip(gather, blocks):
            for i, at in enumerate(table):
                whole = lax.dynamic_update_slice_in_dim(whole, got[i * half : (i + 1) * half], at * half, 0)
        gate = lax.dot_general(gate_weight[0], whole, contract, preferred_element_type=F32)
        up = lax.dot_general(up_weight[0], whole, contract, preferred_element_type=F32)
        hidden = (jax.nn.silu(gate) * up).astype(BF16)
        out = lax.dot_general(down_weight[0], hidden, contract, preferred_element_type=F32).astype(BF16)
        terms = {
            name: cat(*[lax.dynamic_slice_in_dim(out, at * half, half, 0) for at in table])
            for name, table in scatter.items()
        }
        sums.append(scatter_plane(terms, core0))
    summed = jnp.concatenate(sums, axis=1)

    weighted = (summed * share[None, :]).astype(BF16)
    placed = lax.dot_general(weighted, onehot, (((1,), (1,)), ((), ())), preferred_element_type=F32).astype(BF16)
    count = placed.shape[1] // 2
    column = add(placed[:, :count], send(placed[:, count:], (0, 1, 0, 0), (0, 1, 0, 0)))
    column = column.reshape(half, NY, 2 * block)
    got = [column[:, 0]] + [send(column[:, i], my(d), my(d)) for i, d in enumerate(order_y) if i]
    total = sum(v.astype(F32) for v in got).astype(BF16)
    own, other = total[:, :block], lax.ppermute(total[:, block:], "dp", swap_dp)
    return jnp.where(dp == 0, cat(own, other), cat(other, own)).T


def solution(mesh):
    placed = (
        P(("expert", "dp"), "blk"),
        P(("expert", "dp")),
        P("expert", None),
        P("expert", None),
        P("expert", None, ("blk", "dp")),
        P("expert", None, ("blk", "dp")),
        P("expert", ("blk", "dp"), None),
    )
    return jax.shard_map(
        shards, mesh=mesh, in_specs=placed, out_specs=P(("expert", "dp"), "blk"), check_vma=False
    )
```

```python
import functools

import jax
import jax.numpy as jnp
from jax import lax
from jax.experimental import pallas as pl
from jax.experimental.pallas import tpu as pltpu
from jax.sharding import PartitionSpec as P

F32, BF16 = jnp.float32, jnp.bfloat16
AXES = ("expert", "blk", "dp")
NY, NC, NX, NZ = 4, 2, 4, 8
CHUNKS = 2
PARTS = 1


def pairs(move0, move1):
    out = []
    for y in range(NY):
        for c, move in ((0, move0), (1, move1)):
            if move is None:
                continue
            dy, dc, dx, dz = move
            for x in range(NX):
                for z in range(NZ):
                    source = ((y * NC + c) * NX + x) * NZ + z
                    target = (((y + dy) % NY * NC + (c ^ dc)) * NX + (x + dx) % NX) * NZ + (z + dz) % NZ
                    out.append((source, target))
    return out


def send(a, move0, move1):
    return lax.ppermute(a, AXES, pairs(move0, move1))


def mx(d):
    return (0, 0, d, 0)


def mz(d):
    return (0, 0, 0, d)


def my(d):
    return (d, 0, 0, 0)


def cat(*a):
    return jnp.concatenate(a, axis=0)


NEAR = (0, -1, 1, -2)
FAR = (2, -3, 3, 4)


def tables(x, z, core):
    def c0(d):
        return [((x + i) % NX) * NZ + (z + d) % NZ for i in NEAR]

    def c1(d, zs):
        return [((x + d) % NX) * NZ + (z + i) % NZ for i in zs]

    def pick(a, b):
        return [jnp.where(core == 0, p, q) for p, q in zip(a, b)]

    gather = [
        pick(c0(0), c1(0, NEAR)),
        pick(c0(-1), c1(-1, NEAR)),
        pick(c0(1), c1(1, NEAR)),
        pick(c0(-2), c1(-1, FAR)),
        pick(c0(2), c1(1, FAR)),
        pick(c0(-3), c1(2, NEAR)),
        pick(c0(3), c1(2, FAR)),
        pick(c0(4), c1(0, FAR)),
    ]
    scatter = [
        pick(c0(0), c1(0, NEAR)),
        pick(c0(4), c1(0, FAR)),
        pick(c0(3), c1(2, FAR)),
        pick(c0(-3), c1(-1, FAR)),
        pick(c0(2), c1(1, FAR)),
        pick(c0(-2), c1(2, NEAR)),
        pick(c0(1), c1(1, NEAR)),
        pick(c0(-1), c1(-1, NEAR)),
    ]
    return [jnp.stack(sum(table, [])).astype(jnp.int32) for table in (gather, scatter)]


def hold(*a):
    return lax.optimization_barrier(a)


def gather_plane(p, core0, later):
    r1 = send(p, mx(1), mz(1))
    r2 = send(p, mx(-1), mz(-1))
    r3 = send(p, mx(2), mz(2))
    r4 = send(p, None, mz(-2))
    r7 = send(p, mz(4), mz(4))
    f1 = send(jnp.where(core0, r7, r3), mx(1), mz(1))
    f2 = send(jnp.where(core0, r7, r4), mx(-1), mz(-1))
    near = chunks(p, r1, r2, r3)
    a1 = [send(v, mz(1), mx(1)) for v in near]
    b1 = [send(v, mz(-1), mx(-1)) for v in near]
    f3 = send(r7, mx(2), None)
    a1[0], later = hold(a1[0], later)
    last = chunks(jnp.where(core0, r7, r4), f1, f2, jnp.where(core0, f3, r7))
    a2 = [send(jnp.where(core0, u, v), mz(1), mx(1)) for u, v in zip(a1, last)]
    b2 = [send(jnp.where(core0, u, v), mz(-1), mx(-1)) for u, v in zip(b1, last)]
    a3 = [send(jnp.where(core0, u, v), mz(1), mx(1)) for u, v in zip(a2, a1)]
    b3 = [send(v, mz(-1), mx(-1)) for v in b2]
    return [v for block in (near, a1, b1, a2, b2, a3, b3, last) for v in block], later


def chunks(*four):
    step = 4 // CHUNKS
    return [cat(*four[i : i + step]) for i in range(0, 4, step)]


def shard(block, i, n):
    step = 4 // CHUNKS
    return block[i // step][i % step * n : (i % step + 1) * n]


def add(*a):
    total = a[0].astype(F32)
    for v in a[1:]:
        total = total + v.astype(F32)
    return total.astype(BF16)


def scatter_plane(terms, core0):
    n = terms.shape[0] // (NX * NZ)
    size = 4 * n // CHUNKS
    pieces = [terms[size * i : size * (i + 1)] for i in range(8 * CHUNKS)]
    home, last, t1, u1, t2, u2, t3, u3 = [pieces[CHUNKS * i : CHUNKS * (i + 1)] for i in range(8)]
    p1 = [send(v, mz(1), mx(1)) for v in t1]
    m1 = [send(v, mz(-1), mx(-1)) for v in u1]
    p2 = [send(add(u, v), mz(1), mx(1)) for u, v in zip(t2, p1)]
    m2 = [send(add(u, jnp.where(core0, v, 0)), mz(-1), mx(-1)) for u, v in zip(u2, m1)]
    p3 = [send(add(u, jnp.where(core0, v, 0)), mz(1), mx(1)) for u, v in zip(t3, p2)]
    m3 = [send(add(u, v), mz(-1), mx(-1)) for u, v in zip(u3, m2)]
    far = [add(u, jnp.where(core0, 0, v), jnp.where(core0, 0, w)) for u, v, w in zip(last, p2, m1)]
    far = [shard(far, i, n) for i in range(4)]
    f1 = send(far[2], mx(1), mz(1))
    f2 = send(far[1], mx(-1), mz(-1))
    f3 = send(far[3], mx(2), None)
    near = [add(u, v, w) for u, v, w in zip(home, p3, m3)]
    near = [shard(near, i, n) for i in range(4)]
    s1 = send(near[2], mx(1), mz(1))
    s2 = send(near[1], mx(-1), mz(-1))
    s7 = send(jnp.where(core0, add(far[0], f1, f2, f3), far[3]), mz(4), mz(4))
    s3 = send(jnp.where(core0, near[3], add(far[0], f1)), mx(2), mz(2))
    s4 = send(add(near[3], f2), None, mz(-2))
    return sum(v.astype(F32) for v in (near[0], s1, s2, s3, s4, s7))


def expert_kernel(count, order, spots, *refs):
    blocks, (gate_hbm, up_hbm, down_hbm, out), scratch = refs[:-12], refs[-12:-8], refs[-8:]
    whole, weights, down, terms, summed, in_sems, out_sems, weight_sems = scratch
    n = whole.shape[0] // count
    units = gate_hbm.shape[0]
    planes = 4
    each = count // len(blocks)
    per = count // planes
    depth = per * n

    def weight_copies(k):
        cols = pl.ds(k * depth, depth)
        return [
            pltpu.make_async_copy(src.at[:, cols], weights.at[pl.ds(i * units, units), cols], weight_sems.at[2 * k + i])
            for i, src in enumerate((gate_hbm, up_hbm))
        ]

    def in_copy(i):
        rows = pl.ds(pl.multiple_of(order[i] * n, n), n)
        return pltpu.make_async_copy(blocks[i // each].at[pl.ds(i % each * n, n)], whole.at[rows], in_sems.at[i])

    def out_copy(i):
        rows = pl.ds(pl.multiple_of(spots[i] * n, n), n)
        return pltpu.make_async_copy(terms.at[pl.ds(i * n, n)], out.at[rows], out_sems.at[i])

    down_copy = pltpu.make_async_copy(down_hbm, down, weight_sems.at[2 * planes])
    for i in range(count):
        in_copy(i).start()
    for k in range(planes):
        for copy in weight_copies(k):
            copy.start()
    down_copy.start()
    for i in range(count):
        in_copy(i).wait()
    for k in range(planes):
        for copy in weight_copies(k):
            copy.wait()
        cols = slice(k * depth, (k + 1) * depth)
        product = jnp.dot(weights[:, cols], whole[cols, :], preferred_element_type=F32)
        if k == 0:
            summed[...] = product
        else:
            summed[...] += product
    gate = summed[:units, :]
    hidden = (gate / (1.0 + jnp.exp(-gate)) * summed[units:, :]).astype(BF16)
    down_copy.wait()
    for k in range(planes):
        rows = slice(k * depth, (k + 1) * depth)
        terms[rows, :] = jnp.dot(down[rows, :], hidden, preferred_element_type=F32).astype(BF16)
        for i in range(k * per, (k + 1) * per):
            out_copy(i).start()
    for i in range(count):
        out_copy(i).wait()


def expert_layers(order, spots, blocks, gate_rows, up_rows, down_rows):
    count = NX * NZ
    units, model = gate_rows.shape
    width = blocks[0].shape[1]
    smem = pl.BlockSpec(memory_space=pltpu.SMEM)
    anywhere = pl.BlockSpec(memory_space=pl.ANY)
    return pl.pallas_call(
        functools.partial(expert_kernel, count),
        out_shape=jax.ShapeDtypeStruct((model, width), BF16),
        in_specs=[smem, smem] + [anywhere] * (len(blocks) + 3),
        out_specs=anywhere,
        scratch_shapes=[
            pltpu.VMEM((model, width), BF16),
            pltpu.VMEM((2 * units, model), BF16),
            pltpu.VMEM((model, units), BF16),
            pltpu.VMEM((model, width), BF16),
            pltpu.VMEM((2 * units, width), F32),
            pltpu.SemaphoreType.DMA((count,)),
            pltpu.SemaphoreType.DMA((count,)),
            pltpu.SemaphoreType.DMA((9,)),
        ],
        compiler_params=pltpu.CompilerParams(vmem_limit_bytes=44 * 2**20),
        cost_estimate=pl.CostEstimate(
            flops=6 * units * model * width, bytes_accessed=2 * model * (3 * units + 2 * width), transcendentals=units * width
        ),
    )(order, spots, *blocks, gate_rows, up_rows, down_rows)


def shards(tokens, row_scales, chosen, combine, gate_weight, up_weight, down_weight):
    expert = lax.axis_index("expert")
    y, core = expert // NC, expert % NC
    dp = lax.axis_index("dp")
    place = lax.axis_index(("blk", "dp"))
    x, z = place // NZ, place % NZ
    core0 = core == 0
    swap_dp = [(0, 1), (1, 0)]
    block, features = tokens.shape
    half = features // 2
    picks, share = chosen[0], combine[0]
    slots = picks.shape[0]
    width = slots // PARTS
    order_y = (0, -1, 1, 2)

    scaled = (tokens.astype(F32) * row_scales.astype(F32)[:, None]).astype(BF16).T
    mine = lax.dynamic_slice_in_dim(scaled, dp * half, half, 0)
    theirs = lax.dynamic_slice_in_dim(scaled, (1 - dp) * half, half, 0)
    pair = jnp.concatenate([mine, lax.ppermute(theirs, "dp", swap_dp)], axis=1)
    column = jnp.concatenate([pair] + [send(pair, my(-d), my(-d)) for d in order_y[1:]], axis=1)
    rows = jnp.concatenate([column, send(column, (0, 1, 0, 0), (0, 1, 0, 0))], axis=1)
    firsts = [
        ((((y + d) % NY) * NC + (core ^ c)) * 2 + (dp ^ j)) * block
        for c in range(NC)
        for d in order_y
        for j in range(2)
    ]
    ids = (jnp.stack(firsts)[:, None] + jnp.arange(block)[None, :]).reshape(-1)
    onehot = (ids[:, None] == picks[None, :]).astype(BF16)

    gather, scatter = tables(x, z, core)
    shard_ids = jnp.arange(NX * NZ, dtype=jnp.int32)
    spots = jnp.sum(jnp.where(scatter[:, None] == shard_ids[None, :], shard_ids[:, None], 0), axis=0)
    gate_rows, up_rows = gate_weight[0].T, up_weight[0].T
    sums = []
    for part in range(PARTS):
        cols = slice(part * width, (part + 1) * width)
        piece = jnp.dot(rows, onehot[:, cols], preferred_element_type=F32).astype(BF16)
        blocks, down_rows = gather_plane(piece, core0, down_weight[0].T)
        terms = expert_layers(gather, spots, blocks, gate_rows, up_rows, down_rows)
        sums.append(scatter_plane(terms, core0))
    summed = jnp.concatenate(sums, axis=1)

    weighted = (summed * share[None, :]).astype(BF16)
    placed = lax.dot_general(weighted, onehot, (((1,), (1,)), ((), ())), preferred_element_type=F32).astype(BF16)
    count = placed.shape[1] // 2
    column = add(placed[:, :count], send(placed[:, count:], (0, 1, 0, 0), (0, 1, 0, 0)))
    column = column.reshape(half, NY, 2 * block)
    got = [column[:, 0]] + [send(column[:, i], my(d), my(d)) for i, d in enumerate(order_y) if i]
    total = sum(v.astype(F32) for v in got).astype(BF16)
    own, other = total[:, :block], lax.ppermute(total[:, block:], "dp", swap_dp)
    return jnp.where(dp == 0, cat(own, other), cat(other, own)).T


def solution(mesh):
    placed = (
        P(("expert", "dp"), "blk"),
        P(("expert", "dp")),
        P("expert", None),
        P("expert", None),
        P("expert", None, ("blk", "dp")),
        P("expert", None, ("blk", "dp")),
        P("expert", ("blk", "dp"), None),
    )
    return jax.shard_map(
        shards, mesh=mesh, in_specs=placed, out_specs=P(("expert", "dp"), "blk"), check_vma=False
    )
```

```python
import functools

import jax
import jax.numpy as jnp
from jax import lax
from jax.experimental import pallas as pl
from jax.experimental.pallas import tpu as pltpu
from jax.sharding import PartitionSpec as P

F32, BF16 = jnp.float32, jnp.bfloat16
AXES = ("expert", "blk", "dp")
NY, NC, NX, NZ = 4, 2, 4, 8
CHUNKS = 2
PARTS = 1


def pairs(move0, move1):
    out = []
    for y in range(NY):
        for c, move in ((0, move0), (1, move1)):
            if move is None:
                continue
            dy, dc, dx, dz = move
            for x in range(NX):
                for z in range(NZ):
                    source = ((y * NC + c) * NX + x) * NZ + z
                    target = (((y + dy) % NY * NC + (c ^ dc)) * NX + (x + dx) % NX) * NZ + (z + dz) % NZ
                    out.append((source, target))
    return out


def send(a, move0, move1):
    return lax.ppermute(a, AXES, pairs(move0, move1))


def mx(d):
    return (0, 0, d, 0)


def mz(d):
    return (0, 0, 0, d)


def my(d):
    return (d, 0, 0, 0)


def cat(*a):
    return jnp.concatenate(a, axis=0)


NEAR = (0, -1, 1, -2)
FAR = (2, -3, 3, 4)


def tables(x, z, core):
    def c0(d):
        return [((x + i) % NX) * NZ + (z + d) % NZ for i in NEAR]

    def c1(d, zs):
        return [((x + d) % NX) * NZ + (z + i) % NZ for i in zs]

    def pick(a, b):
        return [jnp.where(core == 0, p, q) for p, q in zip(a, b)]

    gather = [
        pick(c0(0), c1(0, NEAR)),
        pick(c0(-1), c1(-1, NEAR)),
        pick(c0(1), c1(1, NEAR)),
        pick(c0(-2), c1(-1, FAR)),
        pick(c0(2), c1(1, FAR)),
        pick(c0(-3), c1(2, NEAR)),
        pick(c0(3), c1(2, FAR)),
        pick(c0(4), c1(0, FAR)),
    ]
    scatter = [
        pick(c0(0), c1(0, NEAR)),
        pick(c0(4), c1(0, FAR)),
        pick(c0(3), c1(2, FAR)),
        pick(c0(-3), c1(-1, FAR)),
        pick(c0(2), c1(1, FAR)),
        pick(c0(-2), c1(2, NEAR)),
        pick(c0(1), c1(1, NEAR)),
        pick(c0(-1), c1(-1, NEAR)),
    ]
    return [jnp.stack(sum(table, [])).astype(jnp.int32) for table in (gather, scatter)]


def hold(*a):
    return lax.optimization_barrier(a)


def gather_plane(p, core0):
    r1 = send(p, mx(1), mz(1))
    r2 = send(p, mx(-1), mz(-1))
    r3 = send(p, mx(2), mz(2))
    r4 = send(p, None, mz(-2))
    r7 = send(p, mz(4), mz(4))
    f1 = send(jnp.where(core0, r7, r3), mx(1), mz(1))
    f2 = send(jnp.where(core0, r7, r4), mx(-1), mz(-1))
    near = chunks(p, r1, r2, r3)
    a1 = [send(v, mz(1), mx(1)) for v in near]
    b1 = [send(v, mz(-1), mx(-1)) for v in near]
    f3 = send(r7, mx(2), None)
    last = chunks(jnp.where(core0, r7, r4), f1, f2, jnp.where(core0, f3, r7))
    a2 = [send(jnp.where(core0, u, v), mz(1), mx(1)) for u, v in zip(a1, last)]
    b2 = [send(jnp.where(core0, u, v), mz(-1), mx(-1)) for u, v in zip(b1, last)]
    a3 = [send(jnp.where(core0, u, v), mz(1), mx(1)) for u, v in zip(a2, a1)]
    b3 = [send(v, mz(-1), mx(-1)) for v in b2]
    return [v for block in (near, a1, b1, a2, b2, a3, b3, last) for v in block]


def chunks(*four):
    step = 4 // CHUNKS
    return [cat(*four[i : i + step]) for i in range(0, 4, step)]


def shard(block, i, n):
    step = 4 // CHUNKS
    return block[i // step][i % step * n : (i % step + 1) * n]


def add(*a):
    total = a[0].astype(F32)
    for v in a[1:]:
        total = total + v.astype(F32)
    return total.astype(BF16)


def scatter_plane(terms, core0):
    n = terms.shape[0] // (NX * NZ)
    size = 4 * n // CHUNKS
    pieces = [terms[size * i : size * (i + 1)] for i in range(8 * CHUNKS)]
    home, last, t1, u1, t2, u2, t3, u3 = [pieces[CHUNKS * i : CHUNKS * (i + 1)] for i in range(8)]
    p1 = [send(v, mz(1), mx(1)) for v in t1]
    m1 = [send(v, mz(-1), mx(-1)) for v in u1]
    p2 = [send(add(u, v), mz(1), mx(1)) for u, v in zip(t2, p1)]
    m2 = [send(add(u, jnp.where(core0, v, 0)), mz(-1), mx(-1)) for u, v in zip(u2, m1)]
    p3 = [send(add(u, jnp.where(core0, v, 0)), mz(1), mx(1)) for u, v in zip(t3, p2)]
    m3 = [send(add(u, v), mz(-1), mx(-1)) for u, v in zip(u3, m2)]
    far = [add(u, jnp.where(core0, 0, v), jnp.where(core0, 0, w)) for u, v, w in zip(last, p2, m1)]
    far = [shard(far, i, n) for i in range(4)]
    f1 = send(far[2], mx(1), mz(1))
    f2 = send(far[1], mx(-1), mz(-1))
    f3 = send(far[3], mx(2), None)
    near = [add(u, v, w) for u, v, w in zip(home, p3, m3)]
    near = [shard(near, i, n) for i in range(4)]
    s1 = send(near[2], mx(1), mz(1))
    s2 = send(near[1], mx(-1), mz(-1))
    s7 = send(jnp.where(core0, add(far[0], f1, f2, f3), far[3]), mz(4), mz(4))
    s3 = send(jnp.where(core0, near[3], add(far[0], f1)), mx(2), mz(2))
    s4 = send(add(near[3], f2), None, mz(-2))
    return sum(v.astype(F32) for v in (near[0], s1, s2, s3, s4, s7))


def expert_kernel(count, order, spots, *refs):
    blocks, (gate_hbm, up_hbm, down_hbm, out), scratch = refs[:-12], refs[-12:-8], refs[-8:]
    whole, weights, down, terms, summed, in_sems, out_sems, weight_sems = scratch
    n = whole.shape[0] // count
    units = gate_hbm.shape[0]
    planes = 4
    each = count // len(blocks)
    per = count // planes
    depth = per * n

    def weight_copies(k):
        cols = pl.ds(k * depth, depth)
        return [
            pltpu.make_async_copy(src.at[:, cols], weights.at[pl.ds(i * units, units), cols], weight_sems.at[2 * k + i])
            for i, src in enumerate((gate_hbm, up_hbm))
        ]

    def in_copy(i):
        rows = pl.ds(pl.multiple_of(order[i] * n, n), n)
        return pltpu.make_async_copy(blocks[i // each].at[pl.ds(i % each * n, n)], whole.at[rows], in_sems.at[i])

    def out_copy(i):
        rows = pl.ds(pl.multiple_of(spots[i] * n, n), n)
        return pltpu.make_async_copy(terms.at[pl.ds(i * n, n)], out.at[rows], out_sems.at[i])

    down_copy = pltpu.make_async_copy(down_hbm, down, weight_sems.at[2 * planes])
    for i in range(count):
        in_copy(i).start()
    for k in range(planes):
        for copy in weight_copies(k):
            copy.start()
    down_copy.start()
    for i in range(count):
        in_copy(i).wait()
    for k in range(planes):
        for copy in weight_copies(k):
            copy.wait()
        cols = slice(k * depth, (k + 1) * depth)
        product = jnp.dot(weights[:, cols], whole[cols, :], preferred_element_type=F32)
        if k == 0:
            summed[...] = product
        else:
            summed[...] += product
    gate = summed[:units, :]
    hidden = (gate / (1.0 + jnp.exp(-gate)) * summed[units:, :]).astype(BF16)
    down_copy.wait()
    for k in range(planes):
        rows = slice(k * depth, (k + 1) * depth)
        terms[rows, :] = lax.dot_general(
            down[:, rows], hidden, (((0,), (0,)), ((), ())), preferred_element_type=F32
        ).astype(BF16)
        for i in range(k * per, (k + 1) * per):
            out_copy(i).start()
    for i in range(count):
        out_copy(i).wait()


def expert_layers(order, spots, blocks, gate_rows, up_rows, down_rows):
    count = NX * NZ
    units, model = gate_rows.shape
    width = blocks[0].shape[1]
    smem = pl.BlockSpec(memory_space=pltpu.SMEM)
    anywhere = pl.BlockSpec(memory_space=pl.ANY)
    return pl.pallas_call(
        functools.partial(expert_kernel, count),
        out_shape=jax.ShapeDtypeStruct((model, width), BF16),
        in_specs=[smem, smem] + [anywhere] * (len(blocks) + 3),
        out_specs=anywhere,
        scratch_shapes=[
            pltpu.VMEM((model, width), BF16),
            pltpu.VMEM((2 * units, model), BF16),
            pltpu.VMEM((units, model), BF16),
            pltpu.VMEM((model, width), BF16),
            pltpu.VMEM((2 * units, width), F32),
            pltpu.SemaphoreType.DMA((count,)),
            pltpu.SemaphoreType.DMA((count,)),
            pltpu.SemaphoreType.DMA((9,)),
        ],
        compiler_params=pltpu.CompilerParams(vmem_limit_bytes=56 * 2**20),
        cost_estimate=pl.CostEstimate(
            flops=6 * units * model * width, bytes_accessed=2 * model * (3 * units + 2 * width), transcendentals=units * width
        ),
    )(order, spots, *blocks, gate_rows, up_rows, down_rows)


def shards(tokens, row_scales, chosen, combine, gate_weight, up_weight, down_weight):
    expert = lax.axis_index("expert")
    y, core = expert // NC, expert % NC
    dp = lax.axis_index("dp")
    place = lax.axis_index(("blk", "dp"))
    x, z = place // NZ, place % NZ
    core0 = core == 0
    swap_dp = [(0, 1), (1, 0)]
    block, features = tokens.shape
    half = features // 2
    picks, share = chosen[0], combine[0]
    slots = picks.shape[0]
    width = slots // PARTS
    order_y = (0, -1, 1, 2)

    scaled = (tokens.astype(F32) * row_scales.astype(F32)[:, None]).astype(BF16).T
    mine = lax.dynamic_slice_in_dim(scaled, dp * half, half, 0)
    theirs = lax.dynamic_slice_in_dim(scaled, (1 - dp) * half, half, 0)
    pair = jnp.concatenate([mine, lax.ppermute(theirs, "dp", swap_dp)], axis=1)
    column = jnp.concatenate([pair] + [send(pair, my(-d), my(-d)) for d in order_y[1:]], axis=1)
    rows = jnp.concatenate([column, send(column, (0, 1, 0, 0), (0, 1, 0, 0))], axis=1)
    firsts = [
        ((((y + d) % NY) * NC + (core ^ c)) * 2 + (dp ^ j)) * block
        for c in range(NC)
        for d in order_y
        for j in range(2)
    ]
    ids = (jnp.stack(firsts)[:, None] + jnp.arange(block)[None, :]).reshape(-1)
    onehot = (ids[:, None] == picks[None, :]).astype(BF16)

    gather, scatter = tables(x, z, core)
    shard_ids = jnp.arange(NX * NZ, dtype=jnp.int32)
    spots = jnp.sum(jnp.where(scatter[:, None] == shard_ids[None, :], shard_ids[:, None], 0), axis=0)
    gate_rows, up_rows, down_rows = gate_weight[0].T, up_weight[0].T, down_weight[0]
    sums = []
    for part in range(PARTS):
        cols = slice(part * width, (part + 1) * width)
        piece = jnp.dot(rows, onehot[:, cols], preferred_element_type=F32).astype(BF16)
        blocks = gather_plane(piece, core0)
        terms = expert_layers(gather, spots, blocks, gate_rows, up_rows, down_rows)
        sums.append(scatter_plane(terms, core0))
    summed = jnp.concatenate(sums, axis=1)

    weighted = (summed * share[None, :]).astype(BF16)
    placed = lax.dot_general(weighted, onehot, (((1,), (1,)), ((), ())), preferred_element_type=F32).astype(BF16)
    count = placed.shape[1] // 2
    column = add(placed[:, :count], send(placed[:, count:], (0, 1, 0, 0), (0, 1, 0, 0)))
    column = column.reshape(half, NY, 2 * block)
    got = [column[:, 0]] + [send(column[:, i], my(d), my(d)) for i, d in enumerate(order_y) if i]
    total = sum(v.astype(F32) for v in got).astype(BF16)
    own, other = total[:, :block], lax.ppermute(total[:, block:], "dp", swap_dp)
    return jnp.where(dp == 0, cat(own, other), cat(other, own)).T


def solution(mesh):
    placed = (
        P(("expert", "dp"), "blk"),
        P(("expert", "dp")),
        P("expert", None),
        P("expert", None),
        P("expert", None, ("blk", "dp")),
        P("expert", None, ("blk", "dp")),
        P("expert", ("blk", "dp"), None),
    )
    return jax.shard_map(
        shards, mesh=mesh, in_specs=placed, out_specs=P(("expert", "dp"), "blk"), check_vma=False
    )
```
